32 devices in a mesh: gx: 4 (over y, x), gy: 8 (over z, core).
Axes of the slice: x: 2, y: 2, z: 4, core: 2. Of those that a mesh axis runs over, the one named last changes fastest.
Arguments:
- plan: int32 [16], replicated, may hold values from 0 to 15, each once
- amplitude: float32 [4, 8, 16, 2, 128], P('gx', 'gy'), may hold values from -12 to 12
- positions: int32 [4, 8, 16, 128], P('gx', 'gy'), may hold values from 0 to 1023
- west_in: bfloat16 [4, 8, 2, 128, 1024], P('gx', 'gy'), may hold values from -6 to 6
- north_in: bfloat16 [4, 8, 2, 128, 1024], P('gx', 'gy'), may hold values from -6 to 6
- corner_now: bfloat16 [4, 8, 2, 128, 128], P('gx', 'gy'), may hold values from -6 to 6
- corner_next: bfloat16 [4, 8, 2, 128, 128], P('gx', 'gy'), may hold values from -6 to 6
- east_map: bfloat16 [4, 8, 2, 1024, 1024], P('gx', 'gy'), may hold values from -0.09375 to 0.09375
- south_map: bfloat16 [4, 8, 2, 1024, 1024], P('gx', 'gy'), may hold values from -0.09375 to 0.09375
Outputs:
- west_out: bfloat16 [4, 8, 2, 128, 1024], P('gx', 'gy')
- north_out: bfloat16 [4, 8, 2, 128, 1024], P('gx', 'gy')
- corner_first: bfloat16 [4, 8, 2, 128, 128], P('gx', 'gy')
- corner_second: bfloat16 [4, 8, 2, 128, 128], P('gx', 'gy')
- interface_residual: float32 [4, 8, 2, 128, 1024], P('gx', 'gy')
The draws below stay inside these ranges and needn't reach their ends.
Inputs may be any that keep to these rules, and one draw needn't show every extreme that they name: `plan`: a permutation of the 16 batches.
All inputs are finite; a program needn't handle non-finite values.
Results may differ from the reference program's by a relative error of at most 0.015.
Values may be sent and summed in bfloat16 or wider, within the bound.
No kernel may reach another device: no remote copies, remote signals or barrier semaphores. Data moves between devices by JAX's collectives and lax.ppermute only.
A program may use at most 64 MiB of HBM per device.

```python
import jax
import jax.numpy as jnp
from jax import lax

M = 1024
K = 128
S = 128
TICKS = 6
NX = 4
NY = 8
NB = 16


def with_ends(array, rng, least, high):
    extent = array.shape
    place = [jax.random.randint(jax.random.fold_in(rng, axis), (), 0, extent[axis]) for axis in range(len(extent))]
    array = array.at[tuple(place)].set(least)
    longest = extent.index(max(extent))
    place[longest] = (place[longest] + 1) % extent[longest]
    return array.at[tuple(place)].set(high)


def block_levels(key, extent, pieces, smallest, high):
    def one(position, parts):
        heights = jax.random.uniform(jax.random.fold_in(jax.random.fold_in(key, 6), position), (parts,), jnp.float32, smallest / len(pieces), high / len(pieces))
        return jnp.repeat(jnp.exp(heights), extent[position] // parts).reshape((-1,) + (1,) * (len(extent) - position - 1))

    factor_of = one(*pieces[0])
    for cut in pieces[1:]:
        factor_of = factor_of * one(*cut)
    return factor_of


def bell_draw(stream_key, dims, width, bound, cuts=(), kind=jnp.bfloat16):
    level = block_levels(stream_key, dims, cuts, -0.22, 0.18) if cuts else 1.0
    entries = jax.random.normal(stream_key, dims, jnp.float32) * width * level
    return jnp.minimum(jnp.maximum(entries, -bound), bound).astype(kind)


def setup_inputs(seed: int = 0) -> dict:
    key_list = jax.random.split(jax.random.key(seed), 10)
    plan = jax.random.permutation(key_list[0], NB).astype(jnp.int32)
    amplitude = bell_draw(key_list[1], (NX, NY, NB, 2, S), 2.0, 12.0, ((0, 4), (1, 8)), jnp.float32)
    positions = with_ends(jax.random.randint(key_list[2], (NX, NY, NB, S), 0, M), jax.random.fold_in(key_list[2], 1), 0, M - 1).astype(jnp.int32)
    west_in = bell_draw(key_list[3], (NX, NY, 2, S, M), 1.0, 6.0, ((0, 4), (1, 8)))
    north_in = bell_draw(key_list[4], (NX, NY, 2, S, M), 1.0, 6.0, ((0, 4), (1, 8)))
    corner_now = bell_draw(key_list[5], (NX, NY, 2, S, K), 1.0, 6.0, ((0, 4), (1, 8)))
    corner_next = bell_draw(key_list[6], (NX, NY, 2, S, K), 1.0, 6.0, ((0, 4), (1, 8)))
    east_map = bell_draw(key_list[7], (NX, NY, 2, M, M), (4 * M) ** -0.5, 0.09375, ((0, 4), (1, 8)))
    south_map = bell_draw(key_list[8], (NX, NY, 2, M, M), (4 * M) ** -0.5, 0.09375, ((0, 4), (1, 8)))
    return {"plan": plan, "amplitude": amplitude, "positions": positions, "west_in": west_in, "north_in": north_in, "corner_now": corner_now, "corner_next": corner_next, "east_map": east_map, "south_map": south_map}


def apply_row(boundary, maps):
    values = boundary.astype(jnp.float32)
    mats = maps.astype(jnp.float32)
    real = jnp.einsum("ysm,ymn->ysn", values[:, 0], mats[:, 0]) - jnp.einsum("ysm,ymn->ysn", values[:, 1], mats[:, 1])
    imag = jnp.einsum("ysm,ymn->ysn", values[:, 0], mats[:, 1]) + jnp.einsum("ysm,ymn->ysn", values[:, 1], mats[:, 0])
    return jnp.stack([real, imag], 1).astype(jnp.bfloat16)


def push_east(field):
    return jnp.concatenate([jnp.zeros_like(field[:1]), field[:-1]], 0)


def push_south(field):
    return jnp.concatenate([jnp.zeros_like(field[:, :1]), field[:, :-1]], 1)


def reference(plan, amplitude, positions, west_in, north_in, corner_now, corner_next, east_map, south_map):
    west, north = west_in, north_in
    corner_a, corner_b = corner_now, corner_next
    column = lax.broadcasted_iota(jnp.int32, (NX, NY), 0)
    row = lax.broadcasted_iota(jnp.int32, (NX, NY), 1)
    boundary = None
    for tick in range(TICKS):
        slot = (tick - column - row + NX + NY - 2).astype(jnp.int32)
        batch = plan[slot]
        amps = jnp.take_along_axis(amplitude, batch[:, :, None, None, None], axis=2)[:, :, 0]
        places = jnp.take_along_axis(positions, batch[:, :, None, None], axis=2)[:, :, 0]
        points = lax.broadcasted_iota(jnp.int32, (NX, NY, S, M), 3)
        onehot = (points == places[:, :, :, None]).astype(jnp.float32)
        total = west.astype(jnp.float32) + north.astype(jnp.float32) + amps[:, :, :, :, None] * onehot[:, :, None]
        padded_corner = jnp.pad(corner_a.astype(jnp.float32), ((0, 0), (0, 0), (0, 0), (0, 0), (0, M - K)))
        boundary = (total + padded_corner).astype(jnp.bfloat16)
        east_out = lax.map(lambda pair: apply_row(pair[0], pair[1]), (boundary, east_map))
        south_out = lax.map(lambda pair: apply_row(pair[0], pair[1]), (boundary, south_map))
        west = push_east(east_out)
        north = push_south(south_out)
        corner_a = corner_b
        corner_b = push_south(push_east(east_out[..., :K]))
    values = boundary.astype(jnp.float32)
    padded = jnp.pad(values, ((1, 1), (1, 1), (0, 0), (0, 0), (0, 0)))
    residual = 4.0 * values - padded[:-2, 1:-1] - padded[2:, 1:-1] - padded[1:-1, :-2] - padded[1:-1, 2:]
    return west, north, corner_a, corner_b, residual
```

```python
import functools

import jax
import jax.numpy as jnp
from jax import lax
from jax.experimental import pallas as pl
from jax.experimental.pallas import tpu as pltpu
from jax.sharding import PartitionSpec as P

TICKS = 6
PARTS = 2
FIELDS = 3
PIECES = 8
VMEM = pl.BlockSpec(memory_space=pltpu.VMEM)
ANY = pl.BlockSpec(memory_space=pl.ANY)
HBM = pl.BlockSpec(memory_space=pltpu.HBM)


COSTS = dict.fromkeys(
    ("east", "south", "last_east0", "last_east1", "middle0", "middle1"), 10**10
)


def kernel_call(name, body, outs, in_specs, out_specs, scratch=()):
    return pl.pallas_call(
        body,
        name=name,
        out_shape=outs,
        in_specs=in_specs,
        out_specs=out_specs,
        scratch_shapes=list(scratch),
        compiler_params=pltpu.CompilerParams(vmem_limit_bytes=24 << 20),
        cost_estimate=pl.CostEstimate(flops=COSTS.get(name, 1000), bytes_accessed=1000, transcendentals=0),
    )


def ring(x, axis, distance):
    size = lax.axis_size(axis)
    return lax.ppermute(x, axis, [(i, (i + distance) % size) for i in range(size)])


def line(x, axis, distance):
    size = lax.axis_size(axis)
    return lax.ppermute(
        x, axis, [(i, i + distance) for i in range(size) if 0 <= i + distance < size]
    )


def inside(axis, towards_end=False):
    here = lax.axis_index(axis)
    there = here < lax.axis_size(axis) - 1 if towards_end else here > 0
    return there.astype(jnp.float32)


def f32(x):
    return x.astype(jnp.float32)


def sources_of(info, tick, rows):
    base = tick * FIELDS
    point = info[rows, base + 2 : base + 3].astype(jnp.int32)

    def spread(part, width):
        points = lax.broadcasted_iota(jnp.int32, (point.shape[0], width), 1)
        return jnp.where(points == point, info[rows, base + part : base + part + 1], 0.0)

    return spread


def stacked(q):
    return jnp.concatenate([q[0], q[1]], 0), jnp.concatenate([-q[1], q[0]], 0)


def product(q, maps):
    ahead, turned = stacked(q)
    out = jnp.dot(ahead, maps[0], preferred_element_type=jnp.float32)
    return out + jnp.dot(turned, maps[1], preferred_element_type=jnp.float32)


def map_copies(source, held, sems):
    depth = held.shape[1] * 2 // PIECES
    copies = []
    for k in range(PIECES):
        half, place = k * 2 // PIECES, pl.ds(k % (PIECES // 2) * depth, depth)
        copies.append(
            pltpu.make_async_copy(source.at[0, 0, half, place], held.at[half, place], sems.at[k])
        )
    return copies


def arriving_product(q, held, copies):
    depth = held.shape[1] * 2 // PIECES
    sides = stacked(q)
    out = None
    for k, copy in enumerate(copies):
        copy.wait()
        half, place = k * 2 // PIECES, k % (PIECES // 2) * depth
        term = jnp.dot(
            sides[half][:, place : place + depth],
            held[half, place : place + depth, :],
            preferred_element_type=jnp.float32,
        )
        out = term if out is None else out + term
    return out


def first_body(
    plan, amplitude, positions, west, north, corner, east_map,
    q0, q1, east, held, info, order, amps, places, w, n, c, table, list_sems, in_sems, map_sems,
):
    step, width = q0.shape[1:]
    corner_width = c.shape[-1]
    lists = [
        pltpu.make_async_copy(plan, order, list_sems.at[0]),
        pltpu.make_async_copy(amplitude.at[0, 0], amps, list_sems.at[1]),
        pltpu.make_async_copy(positions.at[0, 0], places, list_sems.at[2]),
    ]
    traces = []
    for p in range(PARTS):
        cut = pl.ds(p * step, step)
        traces.append(
            [
                pltpu.make_async_copy(west.at[0, 0, :, cut], w.at[:, cut], in_sems.at[p, 0]),
                pltpu.make_async_copy(north.at[0, 0, :, cut], n.at[:, cut], in_sems.at[p, 1]),
                pltpu.make_async_copy(corner.at[0, 0, :, cut], c.at[:, cut], in_sems.at[p, 2]),
            ]
        )
    pieces = map_copies(east_map, held, map_sems)
    for copy in lists + traces[0] + pieces + traces[1]:
        copy.start()
    span = lax.axis_size("gx") + lax.axis_size("gy") - 2
    start = span - lax.axis_index("gx") - lax.axis_index("gy")
    table[...] = jnp.zeros_like(table)
    for copy in lists:
        copy.wait()
    for tick in range(TICKS):
        batch = order[start + tick]
        base = tick * FIELDS
        table[base : base + 2, :] = amps[batch]
        table[base + 2 : base + 3, :] = places[pl.ds(batch, 1), :].astype(jnp.float32)
    info[...] = table[...].T
    for p, q in enumerate((q0, q1)):
        cut = slice(p * step, (p + 1) * step)
        for copy in traces[p]:
            copy.wait()
        spread = sources_of(info, 0, cut)
        for part in range(2):
            total = f32(w[part, cut]) + f32(n[part, cut]) + spread(part, width)
            q[part] = total.astype(q.dtype)
            head = total[:, :corner_width] + f32(c[part, cut])
            q[part, :, :corner_width] = head.astype(q.dtype)
    out = arriving_product(q0[...], held, pieces)
    east[0] = out[:step].astype(east.dtype)
    east[1] = out[step:].astype(east.dtype)


def first_south_body(q, south_map, out, held, map_sems):
    step = q.shape[1]
    pieces = map_copies(south_map, held, map_sems)
    for copy in pieces:
        copy.start()
    total = arriving_product(q[...], held, pieces)
    out[0] = total[:step].astype(out.dtype)
    out[1] = total[step:].astype(out.dtype)


def product_body(q, maps, turn, out):
    step = q.shape[1]
    total = product(q[...], maps)
    out[0] = total[:step].astype(out.dtype)
    out[1] = total[step:].astype(out.dtype)


def east_body(tick, part, w, n, info, maps, corner, turn, q, out):
    step, width = q.shape[1:]
    rows = slice(part * step, (part + 1) * step)
    from_west, from_north = inside("gx"), inside("gy")
    spread = sources_of(info, tick, rows)
    for half in range(2):
        total = f32(w[half]) * from_west + f32(n[half]) * from_north + spread(half, width)
        q[half] = total.astype(q.dtype)
        if corner is not None:
            corner_width = corner.shape[-1]
            head = total[:, :corner_width] + f32(corner[0, 0, half, rows])
            q[half, :, :corner_width] = head.astype(q.dtype)
    total = product(q[...], maps)
    out[0] = total[:step].astype(out.dtype)
    out[1] = total[step:].astype(out.dtype)


def east_plain_body(tick, part, w, n, info, maps, turn, q, out):
    east_body(tick, part, w, n, info, maps, None, turn, q, out)


def south_body(corner_width, q, maps, w, turn, out):
    step = q.shape[1]
    from_west = inside("gx")
    total = product(q[...], maps)
    for half in range(2):
        trace = total[half * step : (half + 1) * step]
        out[half] = trace.astype(out.dtype)
        head = trace[:, :corner_width] + f32(w[half, :, :corner_width]) * from_west
        out[half, :, :corner_width] = head.astype(out.dtype)


def last_south_body(q0, q1, maps, w0, w1, turn, tray):
    step, width = q0.shape[1:]
    from_west = inside("gx")
    for p, (q, w) in enumerate(((q0, w0), (q1, w1))):
        rows = slice(p * step, (p + 1) * step)
        tray[:, rows, width : 2 * width] = q[...]
        corner = f32(w[:, :, : tray.shape[2] - 2 * width]) * from_west
        tray[:, rows, 2 * width :] = corner.astype(tray.dtype)
    total = product(tray[:, :, width : 2 * width], maps)
    for half in range(2):
        trace = total[half * 2 * step : (half + 1) * 2 * step]
        tray[half, :, :width] = trace.astype(tray.dtype)


def first_middle_body(q0, q1, far, west, turn, total, both):
    total[...] = (f32(q0[...]) + f32(far[...])).astype(total.dtype)
    both[:, : q0.shape[1]] = q0[...]
    both[:, q0.shape[1] :] = q1[...]


def middle_body(a, b, w0, w1, turn, total, out, head, whole, sem):
    from_west = inside("gx")
    step = w0.shape[1]
    for p, w in enumerate((w0, w1)):
        whole[:, p * step : (p + 1) * step] = (f32(w[...]) * from_west).astype(whole.dtype)
    copy = pltpu.make_async_copy(whole, out.at[0, 0], sem)
    copy.start()
    head[...] = whole[:, :, : head.shape[-1]]
    total[...] = (f32(a[...]) + f32(b[...])).astype(total.dtype)
    copy.wait()


def base_body(q, tray, down, side, turn, base, first, out, trace, corner, sems):
    width = base.shape[-1]
    from_north, from_south = inside("gy"), inside("gy", True)
    trace[...] = (f32(tray[:, :, :width]) * from_north).astype(trace.dtype)
    corner[...] = (f32(tray[:, :, 2 * width :]) * from_north).astype(corner.dtype)
    copies = [
        pltpu.make_async_copy(trace, out.at[0, 0], sems.at[0]),
        pltpu.make_async_copy(corner, first.at[0, 0], sems.at[1]),
    ]
    for copy in copies:
        copy.start()
    rows = slice(0, side.shape[1])
    for half in range(2):
        base[half] = (
            4.0 * f32(q[half])
            - f32(tray[half, :, width : 2 * width]) * from_north
            - f32(down[half]) * from_south
        )
        base[half, rows] = base[half, rows] - f32(side[half])
    for copy in copies:
        copy.wait()


def final_body(base, side, second, out, corner, rest, held, sems, part_sems):
    held[...] = (f32(second[...]) * inside("gy")).astype(held.dtype)
    step = side.shape[1]
    done, left = pl.ds(0, step), pl.ds(step, step)
    copies = [
        pltpu.make_async_copy(held, corner.at[0, 0], sems.at[0]),
        pltpu.make_async_copy(base.at[:, done], out.at[0, 0, :, done], sems.at[1]),
    ]
    for copy in copies:
        copy.start()
    for half in range(2):
        rest[half] = base[half, step:] - f32(side[half])
        copy = pltpu.make_async_copy(
            rest.at[half], out.at[0, 0, half, left], part_sems.at[half]
        )
        copy.start()
        copies.append(copy)
    for copy in copies:
        copy.wait()


def on_device(
    plan, amplitude, positions, west_in, north_in, corner_now, corner_next, east_map, south_map
):
    columns = lax.axis_size("gx")
    kind = west_in.dtype
    sources, width = west_in.shape[-2:]
    corner_width = corner_now.shape[-1]
    step = sources // PARTS
    part = jax.ShapeDtypeStruct((2, step, width), kind)
    whole = jax.ShapeDtypeStruct((2, sources, width), kind)
    head = jax.ShapeDtypeStruct((2, sources, corner_width), kind)
    maps = jax.ShapeDtypeStruct((2, width, width), kind)
    info = jax.ShapeDtypeStruct((sources, sources), jnp.float32)
    dma = pltpu.SemaphoreType.DMA

    fixed = [
        pltpu.with_memory_space_constraint(x, pltpu.HBM)
        for x in (plan, amplitude, positions, west_in, north_in, corner_now, east_map, south_map)
    ]
    q0, q1, east, east_held, info = kernel_call(
        "first",
        first_body,
        (part, part, part, maps, info),
        [HBM] * 7,
        [VMEM] * 5,
        [
            pltpu.SMEM(plan.shape, plan.dtype),
            pltpu.VMEM(amplitude.shape[2:], amplitude.dtype),
            pltpu.VMEM(positions.shape[2:], positions.dtype),
            pltpu.VMEM((2, sources, width), kind),
            pltpu.VMEM((2, sources, width), kind),
            pltpu.VMEM((2, sources, corner_width), kind),
            pltpu.VMEM((sources, sources), jnp.float32),
            dma((3,)),
            dma((PARTS, 3)),
            dma((PIECES,)),
        ],
    )(*fixed[:-1])
    w0 = ring(east, "gx", 1)
    south, south_held = kernel_call(
        "first_south", first_south_body, (part, maps), [VMEM, HBM], [VMEM] * 2, [dma((PIECES,))]
    )(q0, fixed[-1])
    n0 = ring(south, "gy", 1)
    east = kernel_call("east", product_body, part, [VMEM, VMEM, ANY], VMEM)(q1, east_held, south)
    w1 = ring(east, "gx", 1)
    south = kernel_call("south", product_body, part, [VMEM, VMEM, ANY], VMEM)(q1, south_held, east)
    n1 = ring(south, "gy", 1)
    west, north = [w0, w1], [n0, n1]
    for tick in range(1, TICKS - 1):
        for p in range(PARTS):
            w, n = west[p], north[p]
            if tick == 1:
                q, east = kernel_call(
                    "east", functools.partial(east_body, tick, p), (part, part), [VMEM] * 5 + [ANY], [VMEM] * 2
                )(w, n, info, east_held, corner_next, south)
            else:
                q, east = kernel_call(
                    "east", functools.partial(east_plain_body, tick, p), (part, part), [VMEM] * 4 + [ANY], [VMEM] * 2
                )(w, n, info, east_held, south)
            west[p] = ring(east, "gx", 1)
            south = kernel_call(
                "south", functools.partial(south_body, corner_width), part, [VMEM] * 3 + [ANY], VMEM
            )(q, south_held, w, east)
            north[p] = ring(south, "gy", 1)
    qs, far, last_west, turn = [None] * PARTS, [None] * PARTS, list(west), south
    sends = [(i, i - 2) for i in range(2, columns, 2)] + [(i, i + 2) for i in range(1, columns - 2, 2)]
    for p in range(PARTS):
        qs[p], turn = kernel_call(
            "last_east%d" % p,
            functools.partial(east_plain_body, TICKS - 1, p),
            (part, part),
            [VMEM] * 4 + [ANY],
            [VMEM] * 2,
        )(west[p], north[p], info, east_held, turn)
        west[p] = line(turn, "gx", 1)
        far[p] = lax.ppermute(qs[p], "gx", sends)
    cell = lambda shape, dtype: jax.ShapeDtypeStruct((1, 1) + shape, dtype)
    pairs = [(i, i ^ 1) for i in range(columns)]
    tray = jax.ShapeDtypeStruct((2, sources, 2 * width + corner_width), kind)
    tray = kernel_call("last_south", last_south_body, tray, [VMEM] * 5 + [ANY], VMEM)(
        qs[0], qs[1], south_held, last_west[0], last_west[1], turn
    )
    total, both = kernel_call(
        "middle0", first_middle_body, (part, whole), [VMEM] * 3 + [ANY] * 2, [VMEM] * 2
    )(qs[0], qs[1], far[0], west[0], tray)
    arrived = line(tray, "gy", 1)
    side0 = lax.ppermute(total, "gx", pairs)
    down = line(both, "gy", -1)
    total, west_out, heads = kernel_call(
        "middle1",
        middle_body,
        (part, cell(whole.shape, kind), head),
        [VMEM] * 4 + [ANY],
        [VMEM, HBM, VMEM],
        [pltpu.VMEM(whole.shape, kind), dma(())],
    )(qs[1], far[1], west[0], west[1], total)
    side1 = lax.ppermute(total, "gx", pairs)
    second = ring(heads, "gy", 1)
    base, corner_first, north_out = kernel_call(
        "base",
        base_body,
        (
            jax.ShapeDtypeStruct(whole.shape, jnp.float32),
            cell(head.shape, kind),
            cell(whole.shape, kind),
        ),
        [VMEM] * 4 + [ANY],
        [VMEM, HBM, HBM],
        [pltpu.VMEM(whole.shape, kind), pltpu.VMEM(head.shape, kind), dma((2,))],
    )(both, arrived, down, side0, total)
    residual, corner_second = kernel_call(
        "final",
        final_body,
        (cell(whole.shape, jnp.float32), cell(head.shape, kind)),
        [VMEM] * 3,
        [HBM, HBM],
        [
            pltpu.VMEM(part.shape, jnp.float32),
            pltpu.VMEM(head.shape, kind),
            dma((2,)),
            dma((2,)),
        ],
    )(base, side1, second)
    return west_out, north_out, corner_first, corner_second, residual


def solution(mesh):
    cell = P("gx", "gy")
    return jax.shard_map(
        on_device,
        mesh=mesh,
        in_specs=(P(),) + (cell,) * 8,
        out_specs=(cell,) * 5,
        check_vma=False,
    )
```

```python
import functools

import jax
import jax.numpy as jnp
from jax import lax
from jax.experimental import pallas as pl
from jax.experimental.pallas import tpu as pltpu
from jax.sharding import PartitionSpec as P

TICKS = 6
PARTS = 2
FIELDS = 3
PIECES = 2
VMEM = pl.BlockSpec(memory_space=pltpu.VMEM)
ANY = pl.BlockSpec(memory_space=pl.ANY)
HBM = pl.BlockSpec(memory_space=pltpu.HBM)


COSTS = dict.fromkeys(
    ("first_south", "east", "south", "last_east0", "last_east1", "middle0", "middle1"), 10**10
)


def kernel_call(name, body, outs, in_specs, out_specs, scratch=(), aliases={}):
    return pl.pallas_call(
        body,
        name=name,
        out_shape=outs,
        in_specs=in_specs,
        out_specs=out_specs,
        scratch_shapes=list(scratch),
        input_output_aliases=aliases,
        compiler_params=pltpu.CompilerParams(vmem_limit_bytes=24 << 20),
        cost_estimate=pl.CostEstimate(flops=COSTS.get(name, 1000), bytes_accessed=1000, transcendentals=0),
    )


def ring(x, axis, distance):
    size = lax.axis_size(axis)
    return lax.ppermute(x, axis, [(i, (i + distance) % size) for i in range(size)])


def line(x, axis, distance):
    size = lax.axis_size(axis)
    return lax.ppermute(
        x, axis, [(i, i + distance) for i in range(size) if 0 <= i + distance < size]
    )


def inside(axis, towards_end=False):
    here = lax.axis_index(axis)
    there = here < lax.axis_size(axis) - 1 if towards_end else here > 0
    return there.astype(jnp.float32)


def f32(x):
    return x.astype(jnp.float32)


def sources_of(info, tick, rows):
    base = tick * FIELDS
    point = info[rows, base + 2 : base + 3].astype(jnp.int32)

    def spread(part, width):
        points = lax.broadcasted_iota(jnp.int32, (point.shape[0], width), 1)
        return jnp.where(points == point, info[rows, base + part : base + part + 1], 0.0)

    return spread


def stacked(q):
    return jnp.concatenate([q[0], q[1]], 0), jnp.concatenate([-q[1], q[0]], 0)


def product(q, maps):
    ahead, turned = stacked(q)
    out = jnp.dot(ahead, maps[0], preferred_element_type=jnp.float32)
    return out + jnp.dot(turned, maps[1], preferred_element_type=jnp.float32)


def map_copies(source, held, sems):
    block = held.shape[2] // PIECES
    copies = []
    for k in range(PIECES):
        place = pl.ds(k * block, block)
        copies.append(
            pltpu.make_async_copy(source.at[0, 0, :, :, place], held.at[:, :, place], sems.at[k])
        )
    return copies


def trace_copies(part, step, sources, targets, sems):
    cut = pl.ds(part * step, step)
    return [
        pltpu.make_async_copy(source.at[0, 0, :, cut], target, sems.at[k])
        for k, (source, target) in enumerate(zip(sources, targets))
    ]


def arriving_product(q, held, copies, out):
    step, block = q.shape[1], held.shape[2] // PIECES
    ahead, turned = stacked(q)
    for k, copy in enumerate(copies):
        copy.wait()
        place = slice(k * block, (k + 1) * block)
        total = jnp.dot(ahead, held[0, :, place], preferred_element_type=jnp.float32)
        total = total + jnp.dot(turned, held[1, :, place], preferred_element_type=jnp.float32)
        out[0, :, place] = total[:step].astype(out.dtype)
        out[1, :, place] = total[step:].astype(out.dtype)


def first_boundary(part, info, w, n, c, q):
    step, width = q.shape[1:]
    corner_width = c.shape[-1]
    spread = sources_of(info, 0, slice(part * step, (part + 1) * step))
    for half in range(2):
        total = f32(w[half]) + f32(n[half]) + spread(half, width)
        q[half] = total.astype(q.dtype)
        head = total[:, :corner_width] + f32(c[half])
        q[half, :, :corner_width] = head.astype(q.dtype)


def first_body(
    plan, amplitude, positions, west, north, corner, east_map,
    q, east, held, info, order, amps, places, w, n, c, table, list_sems, trace_sems, map_sems,
):
    lists = [
        pltpu.make_async_copy(plan, order, list_sems.at[0]),
        pltpu.make_async_copy(amplitude.at[0, 0], amps, list_sems.at[1]),
        pltpu.make_async_copy(positions.at[0, 0], places, list_sems.at[2]),
    ]
    traces = trace_copies(0, q.shape[1], (west, north, corner), (w, n, c), trace_sems)
    blocks = map_copies(east_map, held, map_sems)
    for copy in lists + traces + blocks:
        copy.start()
    span = lax.axis_size("gx") + lax.axis_size("gy") - 2
    start = span - lax.axis_index("gx") - lax.axis_index("gy")
    table[...] = jnp.zeros_like(table)
    for copy in lists:
        copy.wait()
    for tick in range(TICKS):
        batch = order[start + tick]
        base = tick * FIELDS
        table[base : base + 2, :] = amps[batch]
        table[base + 2 : base + 3, :] = places[pl.ds(batch, 1), :].astype(jnp.float32)
    info[...] = table[...].T
    for copy in traces:
        copy.wait()
    first_boundary(0, info, w, n, c, q)
    arriving_product(q[...], held, blocks, east)


def first_south_body(q, info, west, north, corner, maps, turn, out, q1, w, n, c, trace_sems):
    step = q.shape[1]
    traces = trace_copies(1, step, (west, north, corner), (w, n, c), trace_sems)
    for copy in traces:
        copy.start()
    total = product(q[...], maps)
    out[0] = total[:step].astype(out.dtype)
    out[1] = total[step:].astype(out.dtype)
    for copy in traces:
        copy.wait()
    first_boundary(1, info, w, n, c, q1)


def last_east_body(part, w, n, info, maps, turn, q, out, first):
    east_body(TICKS - 1, part, w, n, info, maps, None, turn, q, out)
    start = lax.axis_index("gx") == 0

    @pl.when(start)
    def _():
        first[...] = out[...]

    @pl.when(jnp.logical_not(start))
    def _():
        first[...] = q[...]


def product_body(q, maps, turn, out):
    step = q.shape[1]
    total = product(q[...], maps)
    out[0] = total[:step].astype(out.dtype)
    out[1] = total[step:].astype(out.dtype)


def east_body(tick, part, w, n, info, maps, corner, turn, q, out):
    step, width = q.shape[1:]
    rows = slice(part * step, (part + 1) * step)
    from_west, from_north = inside("gx"), inside("gy")
    spread = sources_of(info, tick, rows)
    for half in range(2):
        total = f32(w[half]) * from_west + f32(n[half]) * from_north + spread(half, width)
        q[half] = total.astype(q.dtype)
        if corner is not None:
            corner_width = corner.shape[-1]
            head = total[:, :corner_width] + f32(corner[0, 0, half, rows])
            q[half, :, :corner_width] = head.astype(q.dtype)
    total = product(q[...], maps)
    out[0] = total[:step].astype(out.dtype)
    out[1] = total[step:].astype(out.dtype)


def east_plain_body(tick, part, w, n, info, maps, turn, q, out):
    east_body(tick, part, w, n, info, maps, None, turn, q, out)


def south_body(corner_width, q, maps, w, turn, out):
    step = q.shape[1]
    from_west = inside("gx")
    total = product(q[...], maps)
    for half in range(2):
        trace = total[half * step : (half + 1) * step]
        out[half] = trace.astype(out.dtype)
        head = trace[:, :corner_width] + f32(w[half, :, :corner_width]) * from_west
        out[half, :, :corner_width] = head.astype(out.dtype)


def last_south_body(q0, q1, maps, w0, w1, turn, tray):
    step, width = q0.shape[1:]
    from_west = inside("gx")
    for p, (q, w) in enumerate(((q0, w0), (q1, w1))):
        rows = slice(p * step, (p + 1) * step)
        tray[:, rows, width : 2 * width] = q[...]
        corner = f32(w[:, :, : tray.shape[2] - 2 * width]) * from_west
        tray[:, rows, 2 * width :] = corner.astype(tray.dtype)
    total = product(tray[:, :, width : 2 * width], maps)
    for half in range(2):
        trace = total[half * 2 * step : (half + 1) * 2 * step]
        tray[half, :, :width] = trace.astype(tray.dtype)


def has_far():
    here, size = lax.axis_index("gx"), lax.axis_size("gx")
    there = jnp.where(here % 2 == 0, here + 2, here - 2)
    return ((there >= 0) & (there < size)).astype(jnp.float32)


def first_middle_body(q0, q1, far, west, turn, total, both):
    total[...] = (f32(q0[...]) + f32(far[...]) * has_far()).astype(total.dtype)
    both[:, : q0.shape[1]] = q0[...]
    both[:, q0.shape[1] :] = q1[...]


def middle_body(q, first0, first1, second0, second1, turn, total, out, head, whole, sem):
    here, step = lax.axis_index("gx"), q.shape[1]
    by_first, by_second = (here == 1).astype(jnp.float32), (here > 1).astype(jnp.float32)
    for p, (first, second) in enumerate(((first0, second0), (first1, second1))):
        trace = f32(first[...]) * by_first + f32(second[...]) * by_second
        whole[:, p * step : (p + 1) * step] = trace.astype(whole.dtype)
    copy = pltpu.make_async_copy(whole, out.at[0, 0], sem)
    copy.start()
    head[...] = whole[:, :, : head.shape[-1]]
    total[...] = (f32(q[...]) + f32(first1[...]) * has_far()).astype(total.dtype)
    copy.wait()


def base_body(q, tray, down, side, turn, rest, first, out, residual, trace, corner, done, sems):
    step, width = side.shape[1:]
    from_north, from_south = inside("gy"), inside("gy", True)

    def along_y(half, rows):
        return (
            4.0 * f32(q[half, rows])
            - f32(tray[half, rows, width : 2 * width]) * from_north
            - f32(down[half, rows]) * from_south
        )

    for half in range(2):
        done[half] = along_y(half, slice(0, step)) - f32(side[half])
    trace[...] = (f32(tray[:, :, :width]) * from_north).astype(trace.dtype)
    corner[...] = (f32(tray[:, :, 2 * width :]) * from_north).astype(corner.dtype)
    copies = [
        pltpu.make_async_copy(done, residual.at[0, 0, :, pl.ds(0, step)], sems.at[0]),
        pltpu.make_async_copy(trace, out.at[0, 0], sems.at[1]),
        pltpu.make_async_copy(corner, first.at[0, 0], sems.at[2]),
    ]
    for copy in copies:
        copy.start()
    for half in range(2):
        rest[half] = along_y(half, slice(step, 2 * step))
    for copy in copies:
        copy.wait()


def final_body(base, side, second, begun, out, corner, rest, held, sems):
    step = side.shape[1]
    held[...] = (f32(second[...]) * inside("gy")).astype(held.dtype)
    copies = [pltpu.make_async_copy(held, corner.at[0, 0], sems.at[0])]
    copies[0].start()
    for half in range(2):
        rest[half] = base[half] - f32(side[half])
        copies.append(
            pltpu.make_async_copy(
                rest.at[half], out.at[0, 0, half, pl.ds(step, step)], sems.at[1 + half]
            )
        )
        copies[-1].start()
    for copy in copies:
        copy.wait()


def on_device(
    plan, amplitude, positions, west_in, north_in, corner_now, corner_next, east_map, south_map
):
    columns = lax.axis_size("gx")
    kind = west_in.dtype
    sources, width = west_in.shape[-2:]
    corner_width = corner_now.shape[-1]
    step = sources // PARTS
    part = jax.ShapeDtypeStruct((2, step, width), kind)
    whole = jax.ShapeDtypeStruct((2, sources, width), kind)
    head = jax.ShapeDtypeStruct((2, sources, corner_width), kind)
    maps = jax.ShapeDtypeStruct((2, width, width), kind)
    info = jax.ShapeDtypeStruct((sources, sources), jnp.float32)
    dma = pltpu.SemaphoreType.DMA

    fixed = [
        pltpu.with_memory_space_constraint(x, pltpu.HBM)
        for x in (plan, amplitude, positions, west_in, north_in, corner_now, east_map, south_map)
    ]
    bench = [pltpu.VMEM(part.shape, kind), pltpu.VMEM(part.shape, kind)]
    bench.append(pltpu.VMEM((2, step, corner_width), kind))
    q0, east, east_held, info = kernel_call(
        "first",
        first_body,
        (part, part, maps, info),
        [HBM] * 7,
        [VMEM] * 4,
        [
            pltpu.SMEM(plan.shape, plan.dtype),
            pltpu.VMEM(amplitude.shape[2:], amplitude.dtype),
            pltpu.VMEM(positions.shape[2:], positions.dtype),
            *bench,
            pltpu.VMEM((sources, sources), jnp.float32),
            dma((3,)),
            dma((3,)),
            dma((PIECES,)),
        ],
    )(*fixed[:-1])
    w0 = ring(east, "gx", 1)
    south_held = south_map.reshape(maps.shape)
    south, q1 = kernel_call(
        "first_south",
        first_south_body,
        (part, part),
        [VMEM] * 2 + [HBM] * 3 + [VMEM, ANY],
        [VMEM] * 2,
        [*bench, dma((3,))],
    )(q0, info, *fixed[3:6], south_held, east)
    n0 = ring(south, "gy", 1)
    east = kernel_call("east", product_body, part, [VMEM, VMEM, ANY], VMEM)(q1, east_held, south)
    w1 = ring(east, "gx", 1)
    south = kernel_call("south", product_body, part, [VMEM, VMEM, ANY], VMEM)(q1, south_held, east)
    n1 = ring(south, "gy", 1)
    west, north = [w0, w1], [n0, n1]
    for tick in range(1, TICKS - 1):
        for p in range(PARTS):
            w, n = west[p], north[p]
            if tick == 1:
                q, east = kernel_call(
                    "east", functools.partial(east_body, tick, p), (part, part), [VMEM] * 5 + [ANY], [VMEM] * 2
                )(w, n, info, east_held, corner_next, south)
            else:
                q, east = kernel_call(
                    "east", functools.partial(east_plain_body, tick, p), (part, part), [VMEM] * 4 + [ANY], [VMEM] * 2
                )(w, n, info, east_held, south)
            west[p] = ring(east, "gx", 1)
            south = kernel_call(
                "south", functools.partial(south_body, corner_width), part, [VMEM] * 3 + [ANY], VMEM
            )(q, south_held, w, east)
            north[p] = ring(south, "gy", 1)
    ahead = [(0, 1), (columns - 1, columns - 2)]
    ahead += [(i, i + 2 if i % 2 else i - 2) for i in range(1, columns - 1)]
    rows = lax.axis_size("gy")
    behind = [(j, j ^ 1) for j in range(rows)]
    for i, to in [(columns - 1, 1)] + [(i, i + 1) for i in range(1, columns - 1)]:
        behind += [(i * rows + j, to * rows + j) for j in range(rows)]
    qs, one, two, last_west, turn = [None] * PARTS, [None] * PARTS, [None] * PARTS, list(west), south
    for p in range(PARTS):
        qs[p], turn, first = kernel_call(
            "last_east%d" % p,
            functools.partial(last_east_body, p),
            (part, part, part),
            [VMEM] * 4 + [ANY],
            [VMEM] * 3,
        )(west[p], north[p], info, east_held, turn)
        one[p] = lax.ppermute(first, "gx", ahead)
        two[p] = lax.ppermute(turn, ("gx", "gy"), behind)
    cell = lambda shape, dtype: jax.ShapeDtypeStruct((1, 1) + shape, dtype)
    pairs = [(i, i ^ 1) for i in range(columns)]
    tray = jax.ShapeDtypeStruct((2, sources, 2 * width + corner_width), kind)
    tray = kernel_call("last_south", last_south_body, tray, [VMEM] * 5 + [ANY], VMEM)(
        qs[0], qs[1], south_held, last_west[0], last_west[1], turn
    )
    total, both = kernel_call(
        "middle0", first_middle_body, (part, whole), [VMEM] * 3 + [ANY] * 2, [VMEM] * 2
    )(qs[0], qs[1], one[0], two[0], tray)
    arrived = line(tray, "gy", 1)
    side0 = lax.ppermute(total, "gx", pairs)
    down = line(both, "gy", -1)
    total, west_out, heads = kernel_call(
        "middle1",
        middle_body,
        (part, cell(whole.shape, kind), head),
        [VMEM] * 5 + [ANY],
        [VMEM, HBM, VMEM],
        [pltpu.VMEM(whole.shape, kind), dma(())],
    )(qs[1], one[0], one[1], two[0], two[1], total)
    side1 = lax.ppermute(total, "gx", pairs)
    second = ring(heads, "gy", 1)
    rest = jax.ShapeDtypeStruct(part.shape, jnp.float32)
    rest, corner_first, north_out, residual = kernel_call(
        "base",
        base_body,
        (
            rest,
            cell(head.shape, kind),
            cell(whole.shape, kind),
            cell(whole.shape, jnp.float32),
        ),
        [VMEM] * 4 + [ANY],
        [VMEM, HBM, HBM, HBM],
        [
            pltpu.VMEM(whole.shape, kind),
            pltpu.VMEM(head.shape, kind),
            pltpu.VMEM(rest.shape, rest.dtype),
            dma((3,)),
        ],
    )(both, arrived, down, side0, total)
    residual, corner_second = kernel_call(
        "final",
        final_body,
        (cell(whole.shape, jnp.float32), cell(head.shape, kind)),
        [VMEM] * 3 + [HBM],
        [HBM, HBM],
        [pltpu.VMEM(part.shape, jnp.float32), pltpu.VMEM(head.shape, kind), dma((3,))],
        {3: 0},
    )(rest, side1, second, pltpu.with_memory_space_constraint(residual, pltpu.HBM))
    return west_out, north_out, corner_first, corner_second, residual


def solution(mesh):
    cell = P("gx", "gy")
    return jax.shard_map(
        on_device,
        mesh=mesh,
        in_specs=(P(),) + (cell,) * 8,
        out_specs=(cell,) * 5,
        check_vma=False,
    )
```

```python
import functools

import jax
import jax.numpy as jnp
from jax import lax
from jax.experimental import pallas as pl
from jax.experimental.pallas import tpu as pltpu
from jax.sharding import PartitionSpec as P

TICKS = 6
PARTS = 2
FIELDS = 3
VMEM = pl.BlockSpec(memory_space=pltpu.VMEM)
ANY = pl.BlockSpec(memory_space=pl.ANY)
HBM = pl.BlockSpec(memory_space=pltpu.HBM)


COSTS = dict.fromkeys(
    ("first_south", "east", "south", "last_east0", "early_south", "last_east1", "middle0", "middle1"), 10**10
)


def kernel_call(name, body, outs, in_specs, out_specs, scratch=(), aliases={}):
    return pl.pallas_call(
        body,
        name=name,
        out_shape=outs,
        in_specs=in_specs,
        out_specs=out_specs,
        scratch_shapes=list(scratch),
        input_output_aliases=aliases,
        compiler_params=pltpu.CompilerParams(vmem_limit_bytes=24 << 20),
        cost_estimate=pl.CostEstimate(flops=COSTS.get(name, 1000), bytes_accessed=1000, transcendentals=0),
    )


def ring(x, axis, distance):
    size = lax.axis_size(axis)
    return lax.ppermute(x, axis, [(i, (i + distance) % size) for i in range(size)])


def line(x, axis, distance):
    size = lax.axis_size(axis)
    return lax.ppermute(
        x, axis, [(i, i + distance) for i in range(size) if 0 <= i + distance < size]
    )


def inside(axis, towards_end=False):
    here = lax.axis_index(axis)
    there = here < lax.axis_size(axis) - 1 if towards_end else here > 0
    return there.astype(jnp.float32)


def f32(x):
    return x.astype(jnp.float32)


def sources_of(info, tick, rows):
    base = tick * FIELDS
    point = info[rows, base + 2 : base + 3].astype(jnp.int32)

    def spread(part, width):
        points = lax.broadcasted_iota(jnp.int32, (point.shape[0], width), 1)
        return jnp.where(points == point, info[rows, base + part : base + part + 1], 0.0)

    return spread


def stacked(q):
    return jnp.concatenate([q[0], q[1]], 0), jnp.concatenate([-q[1], q[0]], 0)


def product(q, maps):
    ahead, turned = stacked(q)
    out = jnp.dot(ahead, maps[0], preferred_element_type=jnp.float32)
    return out + jnp.dot(turned, maps[1], preferred_element_type=jnp.float32)


def map_copies(source, held, sems):
    block = held.shape[2] // 2
    left, right = pl.ds(0, block), pl.ds(block, block)
    places = [(pl.ds(0, 2 * block), left), (pl.ds(0, block), right), (pl.ds(block, block), right)]
    return [
        pltpu.make_async_copy(source.at[0, 0, :, rows, cols], held.at[:, rows, cols], sems.at[k])
        for k, (rows, cols) in enumerate(places)
    ]


def trace_copies(part, step, sources, targets, sems):
    cut = pl.ds(part * step, step)
    return [
        pltpu.make_async_copy(source.at[0, 0, :, cut], target, sems.at[k])
        for k, (source, target) in enumerate(zip(sources, targets))
    ]


def arriving_product(q, held, copies, out, part):
    step, block = q.shape[1], held.shape[2] // 2
    ahead, turned = stacked(q)

    def term(rows, cols):
        total = jnp.dot(ahead[:, rows], held[0, rows, cols], preferred_element_type=jnp.float32)
        return total + jnp.dot(turned[:, rows], held[1, rows, cols], preferred_element_type=jnp.float32)

    def put(total, cols):
        out[0, :, cols] = total[:step].astype(out.dtype)
        out[1, :, cols] = total[step:].astype(out.dtype)

    left, right = slice(0, block), slice(block, 2 * block)
    copies[0].wait()
    put(term(slice(0, 2 * block), left), left)
    copies[1].wait()
    part[...] = term(left, right)
    copies[2].wait()
    put(part[...] + term(right, right), right)


def first_boundary(part, info, w, n, c, q):
    step, width = q.shape[1:]
    corner_width = c.shape[-1]
    spread = sources_of(info, 0, slice(part * step, (part + 1) * step))
    for half in range(2):
        total = f32(w[half]) + f32(n[half]) + spread(half, width)
        q[half] = total.astype(q.dtype)
        head = total[:, :corner_width] + f32(c[half])
        q[half, :, :corner_width] = head.astype(q.dtype)


def first_body(
    plan, amplitude, positions, west, north, corner, east_map,
    q, east, held, info, order, amps, places, w, n, c, table, half, list_sems, trace_sems, map_sems,
):
    lists = [
        pltpu.make_async_copy(plan, order, list_sems.at[0]),
        pltpu.make_async_copy(amplitude.at[0, 0], amps, list_sems.at[1]),
        pltpu.make_async_copy(positions.at[0, 0], places, list_sems.at[2]),
    ]
    traces = trace_copies(0, q.shape[1], (west, north, corner), (w, n, c), trace_sems)
    blocks = map_copies(east_map, held, map_sems)
    for copy in lists + traces + blocks:
        copy.start()
    span = lax.axis_size("gx") + lax.axis_size("gy") - 2
    start = span - lax.axis_index("gx") - lax.axis_index("gy")
    table[...] = jnp.zeros_like(table)
    for copy in lists:
        copy.wait()
    for tick in range(TICKS):
        batch = order[start + tick]
        base = tick * FIELDS
        table[base : base + 2, :] = amps[batch]
        table[base + 2 : base + 3, :] = places[pl.ds(batch, 1), :].astype(jnp.float32)
    info[...] = table[...].T
    for copy in traces:
        copy.wait()
    first_boundary(0, info, w, n, c, q)
    arriving_product(q[...], held, blocks, east, half)


def first_south_body(q, info, west, north, corner, maps, turn, out, q1, w, n, c, trace_sems):
    step = q.shape[1]
    traces = trace_copies(1, step, (west, north, corner), (w, n, c), trace_sems)
    for copy in traces:
        copy.start()
    total = product(q[...], maps)
    out[0] = total[:step].astype(out.dtype)
    out[1] = total[step:].astype(out.dtype)
    for copy in traces:
        copy.wait()
    first_boundary(1, info, w, n, c, q1)


def last_east_body(part, w, n, info, maps, turn, q, out, first):
    east_body(TICKS - 1, part, w, n, info, maps, None, turn, q, out)
    start = lax.axis_index("gx") == 0

    @pl.when(start)
    def _():
        first[...] = out[...]

    @pl.when(jnp.logical_not(start))
    def _():
        first[...] = q[...]


def product_body(q, maps, turn, out):
    step = q.shape[1]
    total = product(q[...], maps)
    out[0] = total[:step].astype(out.dtype)
    out[1] = total[step:].astype(out.dtype)


def east_body(tick, part, w, n, info, maps, corner, turn, q, out):
    step, width = q.shape[1:]
    rows = slice(part * step, (part + 1) * step)
    from_west, from_north = inside("gx"), inside("gy")
    spread = sources_of(info, tick, rows)
    for half in range(2):
        total = f32(w[half]) * from_west + f32(n[half]) * from_north + spread(half, width)
        q[half] = total.astype(q.dtype)
        if corner is not None:
            corner_width = corner.shape[-1]
            head = total[:, :corner_width] + f32(corner[0, 0, half, rows])
            q[half, :, :corner_width] = head.astype(q.dtype)
    total = product(q[...], maps)
    out[0] = total[:step].astype(out.dtype)
    out[1] = total[step:].astype(out.dtype)


def east_plain_body(tick, part, w, n, info, maps, turn, q, out):
    east_body(tick, part, w, n, info, maps, None, turn, q, out)


def south_body(corner_width, q, maps, w, turn, out):
    step = q.shape[1]
    from_west = inside("gx")
    total = product(q[...], maps)
    for half in range(2):
        trace = total[half * step : (half + 1) * step]
        out[half] = trace.astype(out.dtype)
        head = trace[:, :corner_width] + f32(w[half, :, :corner_width]) * from_west
        out[half, :, :corner_width] = head.astype(out.dtype)


def early_south_body(q, maps, first, turn, out):
    product_body(q, maps, turn, out)


def last_south_body(q0, q1, south0, maps, w0, w1, turn, tray):
    step, width = q0.shape[1:]
    from_west = inside("gx")
    for p, (q, w) in enumerate(((q0, w0), (q1, w1))):
        rows = slice(p * step, (p + 1) * step)
        tray[:, rows, width : 2 * width] = q[...]
        corner = f32(w[:, :, : tray.shape[2] - 2 * width]) * from_west
        tray[:, rows, 2 * width :] = corner.astype(tray.dtype)
    tray[:, :step, :width] = south0[...]
    total = product(q1[...], maps)
    for half in range(2):
        tray[half, step:, :width] = total[half * step : (half + 1) * step].astype(tray.dtype)


def has_far():
    here, size = lax.axis_index("gx"), lax.axis_size("gx")
    there = jnp.where(here % 2 == 0, here + 2, here - 2)
    return ((there >= 0) & (there < size)).astype(jnp.float32)


def first_middle_body(q0, q1, far, west, turn, total, both):
    total[...] = (f32(q0[...]) + f32(far[...]) * has_far()).astype(total.dtype)
    both[:, : q0.shape[1]] = q0[...]
    both[:, q0.shape[1] :] = q1[...]


def middle_body(q, first0, first1, second0, second1, turn, total, out, head, whole, sem):
    here, step = lax.axis_index("gx"), q.shape[1]
    by_first, by_second = (here == 1).astype(jnp.float32), (here > 1).astype(jnp.float32)
    for p, (first, second) in enumerate(((first0, second0), (first1, second1))):
        trace = f32(first[...]) * by_first + f32(second[...]) * by_second
        whole[:, p * step : (p + 1) * step] = trace.astype(whole.dtype)
    copy = pltpu.make_async_copy(whole, out.at[0, 0], sem)
    copy.start()
    head[...] = whole[:, :, : head.shape[-1]]
    total[...] = (f32(q[...]) + f32(first1[...]) * has_far()).astype(total.dtype)
    copy.wait()


def base_body(q, tray, down, side, turn, rest, first, out, residual, trace, corner, done, sems):
    step, width = side.shape[1:]
    from_north, from_south = inside("gy"), inside("gy", True)

    def along_y(half, rows):
        return (
            4.0 * f32(q[half, rows])
            - f32(tray[half, rows, width : 2 * width]) * from_north
            - f32(down[half, rows]) * from_south
        )

    copies = [
        pltpu.make_async_copy(trace, out.at[0, 0], sems.at[0]),
        pltpu.make_async_copy(done, residual.at[0, 0, :, pl.ds(0, step)], sems.at[1]),
        pltpu.make_async_copy(corner, first.at[0, 0], sems.at[2]),
    ]
    trace[...] = (f32(tray[:, :, :width]) * from_north).astype(trace.dtype)
    copies[0].start()
    for half in range(2):
        done[half] = along_y(half, slice(0, step)) - f32(side[half])
    copies[1].start()
    corner[...] = (f32(tray[:, :, 2 * width :]) * from_north).astype(corner.dtype)
    copies[2].start()
    for half in range(2):
        rest[half] = along_y(half, slice(step, 2 * step))
    for copy in copies:
        copy.wait()


def final_body(base, side, second, begun, out, corner, rest, held, sems):
    step = side.shape[1]
    copies = []
    for half in range(2):
        rest[half] = base[half] - f32(side[half])
        copies.append(
            pltpu.make_async_copy(
                rest.at[half], out.at[0, 0, half, pl.ds(step, step)], sems.at[half]
            )
        )
        copies[half].start()
    held[...] = (f32(second[...]) * inside("gy")).astype(held.dtype)
    copies.append(pltpu.make_async_copy(held, corner.at[0, 0], sems.at[2]))
    copies[2].start()
    for copy in copies:
        copy.wait()


def on_device(
    plan, amplitude, positions, west_in, north_in, corner_now, corner_next, east_map, south_map
):
    columns = lax.axis_size("gx")
    kind = west_in.dtype
    sources, width = west_in.shape[-2:]
    corner_width = corner_now.shape[-1]
    step = sources // PARTS
    part = jax.ShapeDtypeStruct((2, step, width), kind)
    whole = jax.ShapeDtypeStruct((2, sources, width), kind)
    head = jax.ShapeDtypeStruct((2, sources, corner_width), kind)
    maps = jax.ShapeDtypeStruct((2, width, width), kind)
    info = jax.ShapeDtypeStruct((sources, sources), jnp.float32)
    dma = pltpu.SemaphoreType.DMA

    fixed = [
        pltpu.with_memory_space_constraint(x, pltpu.HBM)
        for x in (plan, amplitude, positions, west_in, north_in, corner_now, east_map, south_map)
    ]
    bench = [pltpu.VMEM(part.shape, kind), pltpu.VMEM(part.shape, kind)]
    bench.append(pltpu.VMEM((2, step, corner_width), kind))
    q0, east, east_held, info = kernel_call(
        "first",
        first_body,
        (part, part, maps, info),
        [HBM] * 7,
        [VMEM] * 4,
        [
            pltpu.SMEM(plan.shape, plan.dtype),
            pltpu.VMEM(amplitude.shape[2:], amplitude.dtype),
            pltpu.VMEM(positions.shape[2:], positions.dtype),
            *bench,
            pltpu.VMEM((sources, sources), jnp.float32),
            pltpu.VMEM((2 * step, width // 2), jnp.float32),
            dma((3,)),
            dma((3,)),
            dma((3,)),
        ],
    )(*fixed[:-1])
    w0 = ring(east, "gx", 1)
    south_held = south_map.reshape(maps.shape)
    south, q1 = kernel_call(
        "first_south",
        first_south_body,
        (part, part),
        [VMEM] * 2 + [HBM] * 3 + [VMEM, ANY],
        [VMEM] * 2,
        [*bench, dma((3,))],
    )(q0, info, *fixed[3:6], south_held, east)
    n0 = ring(south, "gy", 1)
    east = kernel_call("east", product_body, part, [VMEM, VMEM, ANY], VMEM)(q1, east_held, south)
    w1 = ring(east, "gx", 1)
    south = kernel_call("south", product_body, part, [VMEM, VMEM, ANY], VMEM)(q1, south_held, east)
    n1 = ring(south, "gy", 1)
    west, north = [w0, w1], [n0, n1]
    for tick in range(1, TICKS - 1):
        for p in range(PARTS):
            w, n = west[p], north[p]
            if tick == 1:
                q, east = kernel_call(
                    "east", functools.partial(east_body, tick, p), (part, part), [VMEM] * 5 + [ANY], [VMEM] * 2
                )(w, n, info, east_held, corner_next, south)
            else:
                q, east = kernel_call(
                    "east", functools.partial(east_plain_body, tick, p), (part, part), [VMEM] * 4 + [ANY], [VMEM] * 2
                )(w, n, info, east_held, south)
            west[p] = ring(east, "gx", 1)
            south = kernel_call(
                "south", functools.partial(south_body, corner_width), part, [VMEM] * 3 + [ANY], VMEM
            )(q, south_held, w, east)
            north[p] = ring(south, "gy", 1)
    ahead = [(0, 1), (columns - 1, columns - 2)]
    ahead += [(i, i + 2 if i % 2 else i - 2) for i in range(1, columns - 1)]
    rows = lax.axis_size("gy")
    behind = [(j, j ^ 1) for j in range(rows)]
    for i, to in [(columns - 1, 1)] + [(i, i + 1) for i in range(1, columns - 1)]:
        behind += [(i * rows + j, to * rows + j) for j in range(rows)]
    qs, one, two, last_west, turn = [None] * PARTS, [None] * PARTS, [None] * PARTS, list(west), south
    for p in range(PARTS):
        qs[p], turn, first = kernel_call(
            "last_east%d" % p,
            functools.partial(last_east_body, p),
            (part, part, part),
            [VMEM] * 4 + [ANY],
            [VMEM] * 3,
        )(west[p], north[p], info, east_held, turn)
        one[p] = lax.ppermute(first, "gx", ahead)
        two[p] = lax.ppermute(turn, ("gx", "gy"), behind)
        if p == 0:
            south0 = turn = kernel_call(
                "early_south", early_south_body, part, [VMEM, VMEM, ANY, ANY], VMEM
            )(qs[0], south_held, first, turn)
    cell = lambda shape, dtype: jax.ShapeDtypeStruct((1, 1) + shape, dtype)
    pairs = [(i, i ^ 1) for i in range(columns)]
    tray = jax.ShapeDtypeStruct((2, sources, 2 * width + corner_width), kind)
    tray = kernel_call("last_south", last_south_body, tray, [VMEM] * 6 + [ANY], VMEM)(
        qs[0], qs[1], south0, south_held, last_west[0], last_west[1], turn
    )
    total, both = kernel_call(
        "middle0", first_middle_body, (part, whole), [VMEM] * 3 + [ANY] * 2, [VMEM] * 2
    )(qs[0], qs[1], one[0], two[0], tray)
    arrived = line(tray, "gy", 1)
    side0 = lax.ppermute(total, "gx", pairs)
    down = line(both, "gy", -1)
    total, west_out, heads = kernel_call(
        "middle1",
        middle_body,
        (part, cell(whole.shape, kind), head),
        [VMEM] * 5 + [ANY],
        [VMEM, HBM, VMEM],
        [pltpu.VMEM(whole.shape, kind), dma(())],
    )(qs[1], one[0], one[1], two[0], two[1], total)
    side1 = lax.ppermute(total, "gx", pairs)
    second = ring(heads, "gy", 1)
    rest = jax.ShapeDtypeStruct(part.shape, jnp.float32)
    rest, corner_first, north_out, residual = kernel_call(
        "base",
        base_body,
        (
            rest,
            cell(head.shape, kind),
            cell(whole.shape, kind),
            cell(whole.shape, jnp.float32),
        ),
        [VMEM] * 4 + [ANY],
        [VMEM, HBM, HBM, HBM],
        [
            pltpu.VMEM(whole.shape, kind),
            pltpu.VMEM(head.shape, kind),
            pltpu.VMEM(rest.shape, rest.dtype),
            dma((3,)),
        ],
    )(both, arrived, down, side0, total)
    residual, corner_second = kernel_call(
        "final",
        final_body,
        (cell(whole.shape, jnp.float32), cell(head.shape, kind)),
        [VMEM] * 3 + [HBM],
        [HBM, HBM],
        [pltpu.VMEM(part.shape, jnp.float32), pltpu.VMEM(head.shape, kind), dma((3,))],
        {3: 0},
    )(rest, side1, second, pltpu.with_memory_space_constraint(residual, pltpu.HBM))
    return west_out, north_out, corner_first, corner_second, residual


def solution(mesh):
    cell = P("gx", "gy")
    return jax.shard_map(
        on_device,
        mesh=mesh,
        in_specs=(P(),) + (cell,) * 8,
        out_specs=(cell,) * 5,
        check_vma=False,
    )
```

```python
import functools

import jax
import jax.numpy as jnp
from jax import lax
from jax.experimental import pallas as pl
from jax.experimental.pallas import tpu as pltpu
from jax.sharding import PartitionSpec as P

TICKS = 6
PARTS = 2
FIELDS = 3
VMEM = pl.BlockSpec(memory_space=pltpu.VMEM)
ANY = pl.BlockSpec(memory_space=pl.ANY)
HBM = pl.BlockSpec(memory_space=pltpu.HBM)


COSTS = dict.fromkeys(
    ("first_south", "pair", "east", "south", "last_east0", "early_south", "last_east1", "middle0", "middle1"), 10**10
)


def kernel_call(name, body, outs, in_specs, out_specs, scratch=(), aliases={}):
    return pl.pallas_call(
        body,
        name=name,
        out_shape=outs,
        in_specs=in_specs,
        out_specs=out_specs,
        scratch_shapes=list(scratch),
        input_output_aliases=aliases,
        compiler_params=pltpu.CompilerParams(vmem_limit_bytes=24 << 20),
        cost_estimate=pl.CostEstimate(flops=COSTS.get(name, 1000), bytes_accessed=1000, transcendentals=0),
    )


def ring(x, axis, distance):
    size = lax.axis_size(axis)
    return lax.ppermute(x, axis, [(i, (i + distance) % size) for i in range(size)])


def line(x, axis, distance):
    size = lax.axis_size(axis)
    return lax.ppermute(
        x, axis, [(i, i + distance) for i in range(size) if 0 <= i + distance < size]
    )


def inside(axis, towards_end=False):
    here = lax.axis_index(axis)
    there = here < lax.axis_size(axis) - 1 if towards_end else here > 0
    return there.astype(jnp.float32)


def f32(x):
    return x.astype(jnp.float32)


def sources_of(info, tick, rows):
    base = tick * FIELDS
    point = info[rows, base + 2 : base + 3].astype(jnp.int32)

    def spread(part, width):
        points = lax.broadcasted_iota(jnp.int32, (point.shape[0], width), 1)
        return jnp.where(points == point, info[rows, base + part : base + part + 1], 0.0)

    return spread


def stacked(q):
    return jnp.concatenate([q[0], q[1]], 0), jnp.concatenate([-q[1], q[0]], 0)


def product(q, maps):
    ahead, turned = stacked(q)
    out = jnp.dot(ahead, maps[0], preferred_element_type=jnp.float32)
    return out + jnp.dot(turned, maps[1], preferred_element_type=jnp.float32)


def map_copies(source, held, sems):
    block = held.shape[2] // 2
    left, right = pl.ds(0, block), pl.ds(block, block)
    places = [(pl.ds(0, 2 * block), left), (pl.ds(0, block), right), (pl.ds(block, block), right)]
    return [
        pltpu.make_async_copy(source.at[0, 0, :, rows, cols], held.at[:, rows, cols], sems.at[k])
        for k, (rows, cols) in enumerate(places)
    ]


def trace_copies(part, step, sources, targets, sems):
    cut = pl.ds(part * step, step)
    return [
        pltpu.make_async_copy(source.at[0, 0, :, cut], target, sems.at[k])
        for k, (source, target) in enumerate(zip(sources, targets))
    ]


def arriving_product(q, held, copies, out, part):
    step, block = q.shape[1], held.shape[2] // 2
    ahead, turned = stacked(q)

    def term(rows, cols):
        total = jnp.dot(ahead[:, rows], held[0, rows, cols], preferred_element_type=jnp.float32)
        return total + jnp.dot(turned[:, rows], held[1, rows, cols], preferred_element_type=jnp.float32)

    def put(total, cols):
        out[0, :, cols] = total[:step].astype(out.dtype)
        out[1, :, cols] = total[step:].astype(out.dtype)

    left, right = slice(0, block), slice(block, 2 * block)
    copies[0].wait()
    put(term(slice(0, 2 * block), left), left)
    copies[1].wait()
    part[...] = term(left, right)
    copies[2].wait()
    put(part[...] + term(right, right), right)


def first_boundary(part, info, w, n, c, q):
    step, width = q.shape[1:]
    corner_width = c.shape[-1]
    spread = sources_of(info, 0, slice(part * step, (part + 1) * step))
    for half in range(2):
        total = f32(w[half]) + f32(n[half]) + spread(half, width)
        q[half] = total.astype(q.dtype)
        head = total[:, :corner_width] + f32(c[half])
        q[half, :, :corner_width] = head.astype(q.dtype)


def first_body(
    plan, amplitude, positions, west, north, corner, east_map,
    q, east, held, info, order, amps, places, w, n, c, table, half, list_sems, trace_sems, map_sems,
):
    lists = [
        pltpu.make_async_copy(plan, order, list_sems.at[0]),
        pltpu.make_async_copy(amplitude.at[0, 0], amps, list_sems.at[1]),
        pltpu.make_async_copy(positions.at[0, 0], places, list_sems.at[2]),
    ]
    traces = trace_copies(0, q.shape[1], (west, north, corner), (w, n, c), trace_sems)
    blocks = map_copies(east_map, held, map_sems)
    for copy in lists + traces + blocks:
        copy.start()
    span = lax.axis_size("gx") + lax.axis_size("gy") - 2
    start = span - lax.axis_index("gx") - lax.axis_index("gy")
    table[...] = jnp.zeros_like(table)
    for copy in lists:
        copy.wait()
    for tick in range(TICKS):
        batch = order[start + tick]
        base = tick * FIELDS
        table[base : base + 2, :] = amps[batch]
        table[base + 2 : base + 3, :] = places[pl.ds(batch, 1), :].astype(jnp.float32)
    info[...] = table[...].T
    for copy in traces:
        copy.wait()
    first_boundary(0, info, w, n, c, q)
    arriving_product(q[...], held, blocks, east, half)


def first_south_body(q, info, west, north, corner, maps, turn, out, q1, w, n, c, trace_sems):
    step = q.shape[1]
    traces = trace_copies(1, step, (west, north, corner), (w, n, c), trace_sems)
    for copy in traces:
        copy.start()
    total = product(q[...], maps)
    out[0] = total[:step].astype(out.dtype)
    out[1] = total[step:].astype(out.dtype)
    for copy in traces:
        copy.wait()
    first_boundary(1, info, w, n, c, q1)


def last_east_body(part, w, n, info, maps, turn, q, out, first):
    east_body(TICKS - 1, part, w, n, info, maps, None, turn, q, out)
    start = lax.axis_index("gx") == 0

    @pl.when(start)
    def _():
        first[...] = out[...]

    @pl.when(jnp.logical_not(start))
    def _():
        first[...] = q[...]


def pair_body(q, east_map, south_map, turn, east, south):
    product_body(q, east_map, turn, east)
    product_body(q, south_map, turn, south)


def product_body(q, maps, turn, out):
    step = q.shape[1]
    total = product(q[...], maps)
    out[0] = total[:step].astype(out.dtype)
    out[1] = total[step:].astype(out.dtype)


def east_body(tick, part, w, n, info, maps, corner, turn, q, out):
    step, width = q.shape[1:]
    rows = slice(part * step, (part + 1) * step)
    from_west, from_north = inside("gx"), inside("gy")
    spread = sources_of(info, tick, rows)
    for half in range(2):
        total = f32(w[half]) * from_west + f32(n[half]) * from_north + spread(half, width)
        q[half] = total.astype(q.dtype)
        if corner is not None:
            corner_width = corner.shape[-1]
            head = total[:, :corner_width] + f32(corner[0, 0, half, rows])
            q[half, :, :corner_width] = head.astype(q.dtype)
    total = product(q[...], maps)
    out[0] = total[:step].astype(out.dtype)
    out[1] = total[step:].astype(out.dtype)


def east_plain_body(tick, part, w, n, info, maps, turn, q, out):
    east_body(tick, part, w, n, info, maps, None, turn, q, out)


def south_body(corner_width, q, maps, w, turn, out):
    step = q.shape[1]
    from_west = inside("gx")
    total = product(q[...], maps)
    for half in range(2):
        trace = total[half * step : (half + 1) * step]
        out[half] = trace.astype(out.dtype)
        head = trace[:, :corner_width] + f32(w[half, :, :corner_width]) * from_west
        out[half, :, :corner_width] = head.astype(out.dtype)


def early_south_body(q, maps, first, turn, out):
    product_body(q, maps, turn, out)


def last_south_body(q0, q1, south0, maps, w0, w1, turn, tray):
    step, width = q0.shape[1:]
    from_west = inside("gx")
    for p, (q, w) in enumerate(((q0, w0), (q1, w1))):
        rows = slice(p * step, (p + 1) * step)
        tray[:, rows, width : 2 * width] = q[...]
        corner = f32(w[:, :, : tray.shape[2] - 2 * width]) * from_west
        tray[:, rows, 2 * width :] = corner.astype(tray.dtype)
    tray[:, :step, :width] = south0[...]
    total = product(q1[...], maps)
    for half in range(2):
        tray[half, step:, :width] = total[half * step : (half + 1) * step].astype(tray.dtype)


def has_far():
    here, size = lax.axis_index("gx"), lax.axis_size("gx")
    there = jnp.where(here % 2 == 0, here + 2, here - 2)
    return ((there >= 0) & (there < size)).astype(jnp.float32)


def first_middle_body(q0, q1, far, west, turn, total, both):
    total[...] = (f32(q0[...]) + f32(far[...]) * has_far()).astype(total.dtype)
    both[:, : q0.shape[1]] = q0[...]
    both[:, q0.shape[1] :] = q1[...]


def middle_body(q, first0, first1, second0, second1, turn, total, out, head, whole, sem):
    here, step = lax.axis_index("gx"), q.shape[1]
    by_first, by_second = (here == 1).astype(jnp.float32), (here > 1).astype(jnp.float32)
    for p, (first, second) in enumerate(((first0, second0), (first1, second1))):
        trace = f32(first[...]) * by_first + f32(second[...]) * by_second
        whole[:, p * step : (p + 1) * step] = trace.astype(whole.dtype)
    copy = pltpu.make_async_copy(whole, out.at[0, 0], sem)
    copy.start()
    head[...] = whole[:, :, : head.shape[-1]]
    total[...] = (f32(q[...]) + f32(first1[...]) * has_far()).astype(total.dtype)
    copy.wait()


def base_body(q, tray, down, side, turn, rest, first, out, residual, trace, corner, done, sems):
    step, width = side.shape[1:]
    from_north, from_south = inside("gy"), inside("gy", True)

    def along_y(half, rows):
        return (
            4.0 * f32(q[half, rows])
            - f32(tray[half, rows, width : 2 * width]) * from_north
            - f32(down[half, rows]) * from_south
        )

    copies = [
        pltpu.make_async_copy(trace, out.at[0, 0], sems.at[0]),
        pltpu.make_async_copy(done, residual.at[0, 0, :, pl.ds(0, step)], sems.at[1]),
        pltpu.make_async_copy(corner, first.at[0, 0], sems.at[2]),
    ]
    trace[...] = (f32(tray[:, :, :width]) * from_north).astype(trace.dtype)
    copies[0].start()
    for half in range(2):
        done[half] = along_y(half, slice(0, step)) - f32(side[half])
    copies[1].start()
    corner[...] = (f32(tray[:, :, 2 * width :]) * from_north).astype(corner.dtype)
    copies[2].start()
    for half in range(2):
        rest[half] = along_y(half, slice(step, 2 * step))
    for copy in copies:
        copy.wait()


def final_body(base, side, second, begun, out, corner, rest, held, sems):
    step = side.shape[1]
    copies = []
    for half in range(2):
        rest[half] = base[half] - f32(side[half])
        copies.append(
            pltpu.make_async_copy(
                rest.at[half], out.at[0, 0, half, pl.ds(step, step)], sems.at[half]
            )
        )
        copies[half].start()
    held[...] = (f32(second[...]) * inside("gy")).astype(held.dtype)
    copies.append(pltpu.make_async_copy(held, corner.at[0, 0], sems.at[2]))
    copies[2].start()
    for copy in copies:
        copy.wait()


def on_device(
    plan, amplitude, positions, west_in, north_in, corner_now, corner_next, east_map, south_map
):
    columns = lax.axis_size("gx")
    kind = west_in.dtype
    sources, width = west_in.shape[-2:]
    corner_width = corner_now.shape[-1]
    step = sources // PARTS
    part = jax.ShapeDtypeStruct((2, step, width), kind)
    whole = jax.ShapeDtypeStruct((2, sources, width), kind)
    head = jax.ShapeDtypeStruct((2, sources, corner_width), kind)
    maps = jax.ShapeDtypeStruct((2, width, width), kind)
    info = jax.ShapeDtypeStruct((sources, sources), jnp.float32)
    dma = pltpu.SemaphoreType.DMA

    fixed = [
        pltpu.with_memory_space_constraint(x, pltpu.HBM)
        for x in (plan, amplitude, positions, west_in, north_in, corner_now, east_map, south_map)
    ]
    bench = [pltpu.VMEM(part.shape, kind), pltpu.VMEM(part.shape, kind)]
    bench.append(pltpu.VMEM((2, step, corner_width), kind))
    q0, east, east_held, info = kernel_call(
        "first",
        first_body,
        (part, part, maps, info),
        [HBM] * 7,
        [VMEM] * 4,
        [
            pltpu.SMEM(plan.shape, plan.dtype),
            pltpu.VMEM(amplitude.shape[2:], amplitude.dtype),
            pltpu.VMEM(positions.shape[2:], positions.dtype),
            *bench,
            pltpu.VMEM((sources, sources), jnp.float32),
            pltpu.VMEM((2 * step, width // 2), jnp.float32),
            dma((3,)),
            dma((3,)),
            dma((3,)),
        ],
    )(*fixed[:-1])
    w0 = ring(east, "gx", 1)
    south_held = south_map.reshape(maps.shape)
    south, q1 = kernel_call(
        "first_south",
        first_south_body,
        (part, part),
        [VMEM] * 2 + [HBM] * 3 + [VMEM, ANY],
        [VMEM] * 2,
        [*bench, dma((3,))],
    )(q0, info, *fixed[3:6], south_held, east)
    n0 = ring(south, "gy", 1)
    east, south = kernel_call("pair", pair_body, (part, part), [VMEM] * 3 + [ANY], [VMEM] * 2)(
        q1, east_held, south_held, south
    )
    w1, n1 = ring(east, "gx", 1), ring(south, "gy", 1)
    west, north = [w0, w1], [n0, n1]
    for tick in range(1, TICKS - 1):
        for p in range(PARTS):
            w, n = west[p], north[p]
            if tick == 1:
                q, east = kernel_call(
                    "east", functools.partial(east_body, tick, p), (part, part), [VMEM] * 5 + [ANY], [VMEM] * 2
                )(w, n, info, east_held, corner_next, south)
            else:
                q, east = kernel_call(
                    "east", functools.partial(east_plain_body, tick, p), (part, part), [VMEM] * 4 + [ANY], [VMEM] * 2
                )(w, n, info, east_held, south)
            west[p] = ring(east, "gx", 1)
            south = kernel_call(
                "south", functools.partial(south_body, corner_width), part, [VMEM] * 3 + [ANY], VMEM
            )(q, south_held, w, east)
            north[p] = ring(south, "gy", 1)
    ahead = [(0, 1), (columns - 1, columns - 2)]
    ahead += [(i, i + 2 if i % 2 else i - 2) for i in range(1, columns - 1)]
    rows = lax.axis_size("gy")
    behind = [(j, j ^ 1) for j in range(rows)]
    for i, to in [(columns - 1, 1)] + [(i, i + 1) for i in range(1, columns - 1)]:
        behind += [(i * rows + j, to * rows + j) for j in range(rows)]
    qs, one, two, last_west, turn = [None] * PARTS, [None] * PARTS, [None] * PARTS, list(west), south
    for p in range(PARTS):
        qs[p], turn, first = kernel_call(
            "last_east%d" % p,
            functools.partial(last_east_body, p),
            (part, part, part),
            [VMEM] * 4 + [ANY],
            [VMEM] * 3,
        )(west[p], north[p], info, east_held, turn)
        one[p] = lax.ppermute(first, "gx", ahead)
        two[p] = lax.ppermute(turn, ("gx", "gy"), behind)
        if p == 0:
            south0 = turn = kernel_call(
                "early_south", early_south_body, part, [VMEM, VMEM, ANY, ANY], VMEM
            )(qs[0], south_held, first, turn)
    cell = lambda shape, dtype: jax.ShapeDtypeStruct((1, 1) + shape, dtype)
    pairs = [(i, i ^ 1) for i in range(columns)]
    tray = jax.ShapeDtypeStruct((2, sources, 2 * width + corner_width), kind)
    tray = kernel_call("last_south", last_south_body, tray, [VMEM] * 6 + [ANY], VMEM)(
        qs[0], qs[1], south0, south_held, last_west[0], last_west[1], turn
    )
    total, both = kernel_call(
        "middle0", first_middle_body, (part, whole), [VMEM] * 3 + [ANY] * 2, [VMEM] * 2
    )(qs[0], qs[1], one[0], two[0], tray)
    arrived = line(tray, "gy", 1)
    side0 = lax.ppermute(total, "gx", pairs)
    down = line(both, "gy", -1)
    total, west_out, heads = kernel_call(
        "middle1",
        middle_body,
        (part, cell(whole.shape, kind), head),
        [VMEM] * 5 + [ANY],
        [VMEM, HBM, VMEM],
        [pltpu.VMEM(whole.shape, kind), dma(())],
    )(qs[1], one[0], one[1], two[0], two[1], total)
    side1 = lax.ppermute(total, "gx", pairs)
    second = ring(heads, "gy", 1)
    rest = jax.ShapeDtypeStruct(part.shape, jnp.float32)
    rest, corner_first, north_out, residual = kernel_call(
        "base",
        base_body,
        (
            rest,
            cell(head.shape, kind),
            cell(whole.shape, kind),
            cell(whole.shape, jnp.float32),
        ),
        [VMEM] * 4 + [ANY],
        [VMEM, HBM, HBM, HBM],
        [
            pltpu.VMEM(whole.shape, kind),
            pltpu.VMEM(head.shape, kind),
            pltpu.VMEM(rest.shape, rest.dtype),
            dma((3,)),
        ],
    )(both, arrived, down, side0, total)
    residual, corner_second = kernel_call(
        "final",
        final_body,
        (cell(whole.shape, jnp.float32), cell(head.shape, kind)),
        [VMEM] * 3 + [HBM],
        [HBM, HBM],
        [pltpu.VMEM(part.shape, jnp.float32), pltpu.VMEM(head.shape, kind), dma((3,))],
        {3: 0},
    )(rest, side1, second, pltpu.with_memory_space_constraint(residual, pltpu.HBM))
    return west_out, north_out, corner_first, corner_second, residual


def solution(mesh):
    cell = P("gx", "gy")
    return jax.shard_map(
        on_device,
        mesh=mesh,
        in_specs=(P(),) + (cell,) * 8,
        out_specs=(cell,) * 5,
        check_vma=False,
    )
```
